32 devices in a mesh: ctx: 16 (over z, x, core), head: 2 (over y).
Axes of the slice: x: 2, y: 2, z: 4, core: 2. Of those that a mesh axis runs over, the one named last changes fastest.
Arguments:
- queries: bfloat16 [2048, 6144], P('ctx', 'head'), as said below
- keys: bfloat16 [4096, 1024], P('ctx', 'head'), as said below
- values: bfloat16 [4096, 1024], P('ctx', 'head'), may hold values from -6 to 6
- ranges: int32 [4, 2, 2], replicated, may hold values from 0 to 32, as said below
- noise_ids: int32 [4], replicated, may hold values from 0 to 7
- block_position: int32 [32], replicated, may hold values from 0 to 31, as said below
- level_gain: float32 [8, 6144], P(None, 'head'), may hold values from 0.1 to 1.9
Outputs:
- attended: bfloat16 [2048, 6144], P('ctx', 'head')
The draws below stay inside these ranges and needn't reach their ends.
Inputs may be any that keep to these rules, and one draw needn't show every extreme that they name: block_position is a permutation of 0 to 31. Each range has start < end and spans 1 to 16 blocks; some range spans exactly 16; ranges of a stretch may intersect. `queries`: entries of order one in most rows; a draw may hold a few rows whose entries are up to about 28 times larger. `keys`: entries of order one.
All inputs are finite; a program needn't handle non-finite values.
Results may differ from the reference program's by a relative error of at most 0.0075.
Values may be sent and summed in bfloat16 or wider, within the bound.
No kernel may reach another device: no remote copies, remote signals or barrier semaphores. Data moves between devices by JAX's collectives and lax.ppermute only.
A program may use at most 64 MiB of HBM per device.

```python
import jax
import jax.numpy as jnp
from jax import lax

D = 6144
KVH = 8
HD = 128
BLK = 128
STRETCHES = 4
NR = 2
LEVELS = 8
GROUP = 6
QTOK = 2048
KTOK = 4096
KBLOCKS = 32
QC = 512
RSPAN = 16


def make_ranges(key):
    first, second = jax.random.split(jax.random.fold_in(key, 11))
    starts = jax.random.randint(first, (STRETCHES, NR), 0, KBLOCKS - RSPAN + 1)
    spans = jax.random.randint(second, (STRETCHES, NR), 1, RSPAN + 1)
    result = jnp.stack([starts, starts + spans], axis=-1).astype(jnp.int32)
    result = result.at[0, 0].set(jnp.array([0, RSPAN], jnp.int32))
    result = result.at[STRETCHES - 1, NR - 1].set(jnp.array([KBLOCKS - RSPAN, KBLOCKS], jnp.int32))
    return result


def make_positions(key):
    return jax.random.permutation(jax.random.fold_in(key, 12), KBLOCKS).astype(jnp.int32)


def make_pair(key):
    key_base = jnp.clip(jax.random.normal(jax.random.fold_in(key, 13), (KTOK, KVH * HD), jnp.float32), -6.0, 6.0)
    query_base = jnp.clip(jax.random.normal(jax.random.fold_in(key, 14), (QTOK, D), jnp.float32), -6.0, 6.0)
    return (query_base, key_base)


def draw_queries(key, part):
    return make_pair(key)[0].astype(jnp.bfloat16)


def draw_keys(key, part):
    return make_pair(key)[1].astype(jnp.bfloat16)


def draw_ranges(key, part):
    return make_ranges(key)


def draw_block_position(key, part):
    return make_positions(key)


def with_ends(entries, own_key, least, high):
    longest = entries.shape.index(max(entries.shape))
    spots = []
    for shift in (0, 1):
        where = [jax.random.randint(jax.random.fold_in(own_key, axis), (), 0, length) for axis, length in enumerate(entries.shape)]
        where[longest] = (where[longest] + shift) % entries.shape[longest]
        spots.append(tuple(where))
    return entries.at[spots[0]].set(least).at[spots[1]].set(high)


def shard_levels(key, extent, pieces, least, high):
    factor_of = 1.0
    for axis_at, blocks in pieces:
        heights = jax.random.uniform(jax.random.fold_in(jax.random.fold_in(key, 6), axis_at), (blocks,), jnp.float32, least / len(pieces), high / len(pieces))
        factor_of = factor_of * jnp.repeat(jnp.exp(heights), extent[axis_at] // blocks).reshape((-1,) + (1,) * (len(extent) - 1 - axis_at))
    return factor_of


def centred(stream_key, extent, width, reach, shards=(), kind=jnp.bfloat16):
    values = jax.random.normal(stream_key, extent, jnp.float32) * width
    if len(shards) > 0:
        values = shard_levels(stream_key, extent, shards, -0.22, 0.18) * values
    return jnp.clip(values, min=-reach, max=reach).astype(kind)


def setup_inputs(seed: int = 0) -> dict:
    splits = jax.random.split(jax.random.key(seed), 8)
    queries = draw_queries(jax.random.fold_in(splits[7], 71), 0)
    keys = draw_keys(jax.random.fold_in(splits[7], 71), 0)
    values = centred(splits[2], (KTOK, KVH * HD), 1.0, 6.0, ((0, 16), (1, 2)))
    ranges = draw_ranges(jax.random.fold_in(splits[7], 71), 0)
    noise_ids = with_ends(jax.random.randint(splits[4], (STRETCHES,), 0, LEVELS), jax.random.fold_in(splits[4], 1), 0, LEVELS - 1).astype(jnp.int32)
    block_position = draw_block_position(jax.random.fold_in(splits[7], 71), 0)
    level_gain = jnp.clip(1.0 + 0.18 * jax.random.normal(splits[6], (LEVELS, D), jnp.float32), 0.1, 1.9)
    return dict(queries=queries, keys=keys, values=values, ranges=ranges, noise_ids=noise_ids, block_position=block_position, level_gain=level_gain)


def reference(queries, keys, values, ranges, noise_ids, block_position, level_gain):
    score_scale = 1.0 / HD ** 0.5
    logical = block_position[jnp.arange(KTOK) // BLK]
    live_all = jnp.any((logical[None, None, :] >= ranges[:, :, 0:1]) & (logical[None, None, :] < ranges[:, :, 1:2]), axis=1)
    q_block = min(512, QC)
    n_blocks = QTOK // q_block
    keys_heads = keys.reshape(KTOK, KVH, HD).transpose(1, 0, 2)
    values_heads = values.reshape(KTOK, KVH, HD).transpose(1, 0, 2)

    def one_block(index):
        rows = lax.dynamic_slice_in_dim(queries, (index * q_block).astype(jnp.int32), q_block, 0)
        rows = rows.reshape(q_block, KVH, GROUP, HD).transpose(1, 0, 2, 3).reshape(KVH, q_block * GROUP, HD)
        stretch = index * q_block // QC
        live_keys = live_all[stretch]

        def one_head(items):
            query_rows, key_rows, value_rows = items
            score = jnp.dot(query_rows, key_rows.T, preferred_element_type=jnp.float32) * score_scale
            score = jnp.where(live_keys[None, :], score, -1e+30)
            top = lax.optimization_barrier(jnp.max(score, axis=1, keepdims=True))
            weight = jnp.exp(score - top)
            total = lax.optimization_barrier(jnp.sum(weight, axis=1, keepdims=True))
            weight_bf = weight.astype(jnp.bfloat16)
            summed = jnp.dot(weight_bf, value_rows, preferred_element_type=jnp.float32)
            return summed / total
        heads = lax.map(one_head, (rows, keys_heads, values_heads))
        heads = heads.reshape(KVH, q_block, GROUP, HD).transpose(1, 0, 2, 3).reshape(q_block, D)
        square = lax.optimization_barrier(jnp.sum(heads * heads, axis=1, keepdims=True))
        gain_row = level_gain[noise_ids[stretch]]
        return (heads / jnp.sqrt(square / D + 1e-06) * gain_row[None, :]).astype(jnp.bfloat16)
    blocks = lax.map(one_block, jnp.arange(n_blocks, dtype=jnp.int32))
    return blocks.reshape(QTOK, D)
```

```python
import functools

import jax
import jax.numpy as jnp
from jax import lax
from jax.experimental import pallas as pl
from jax.experimental.pallas import tpu as pltpu
from jax.sharding import PartitionSpec as P

D = 6144
HD = 128
BLK = 128
STRETCHES = 4
LEVELS = 8
LOG2E = 1.4426950408889634
NEGATIVE = -1e30

F32 = jnp.float32
BF16 = jnp.bfloat16
VMEM = pl.BlockSpec(memory_space=pltpu.VMEM)
SMEM = pl.BlockSpec(memory_space=pltpu.SMEM)
ROOM = 56 * 1024 * 1024


def attend_kernel(spec, *refs):
    sources, split, per_device, group_size, first, last, nr = spec
    where_ref, ranges_ref, position_ref, q_ref = refs[:4]
    at = 4
    key_refs, value_refs = refs[at : at + sources], refs[at + sources : at + 2 * sources]
    at += 2 * sources
    if not first:
        acc_in, stat_in = refs[at : at + 2]
        at += 2
    if last:
        out_ref = refs[at]
        at += 1
    else:
        acc_out, stat_out = refs[at : at + 2]
        at += 2
    kept_k, kept_v, score_ref, acc_ref, count_ref = refs[at : at + 5]
    q_rows = q_ref.shape[1]
    width = q_rows * group_size
    to_log2 = LOG2E / HD**0.5

    @pl.when(pl.program_id(0) == 0)
    def _():
        place, stretch = where_ref[0], where_ref[1]
        count = jnp.int32(0)
        for source in range(sources):
            group = where_ref[2 + source]
            held = jnp.maximum(group, 0)
            for step in range(split):
                device = held * split + jnp.bitwise_xor(place, step)
                for block in range(per_device):
                    logical = position_ref[device * per_device + block]
                    live = jnp.bool_(False)
                    for r in range(nr):
                        low = ranges_ref[(stretch * nr + r) * 2]
                        high = ranges_ref[(stretch * nr + r) * 2 + 1]
                        live = live | ((logical >= low) & (logical < high))
                    live = live & (group >= 0)
                    slot = step * per_device + block

                    @pl.when(live)
                    def _(count=count, source=source, slot=slot):
                        kept_k[count] = key_refs[source][slot]
                        kept_v[count] = value_refs[source][slot]

                    count = count + live.astype(jnp.int32)
        count_ref[0] = count
        kept_v[count] = jnp.zeros((BLK, HD), BF16)

    count = count_ref[0]
    pairs = lax.div(count, 2)
    q = jnp.concatenate([q_ref[0, :, g * HD : (g + 1) * HD] for g in range(group_size)], axis=0)

    def pair_scores(index, top):
        keys = kept_k[pl.ds(index * 2, 2)].reshape(2 * BLK, HD)
        score = lax.dot_general(q, keys, (((1,), (1,)), ((), ())), preferred_element_type=F32)
        score_ref[index] = score
        return jnp.maximum(top, jnp.maximum(score[:, :BLK], score[:, BLK:]))

    top = lax.fori_loop(0, pairs, pair_scores, jnp.full((width, BLK), NEGATIVE, F32))
    acc_ref[:, :HD] = top

    @pl.when(count > pairs * 2)
    def _():
        keys = kept_k[count - 1]
        score = lax.dot_general(q, keys, (((1,), (1,)), ((), ())), preferred_element_type=F32)
        score_ref[pairs, :, :BLK] = score
        score_ref[pairs, :, BLK:] = jnp.full((width, BLK), NEGATIVE, F32)
        acc_ref[:, :HD] = jnp.maximum(acc_ref[:, :HD], score)

    top = jnp.max(acc_ref[:, :HD], axis=1, keepdims=True) * to_log2
    if not first:
        old_top = stat_in[0, :, :1]
        top = jnp.maximum(top, old_top)
        correct = jnp.exp2(old_top - top)
        acc_ref[:, :HD] = acc_in[0] * correct
        acc_ref[:, HD:] = jnp.broadcast_to(stat_in[0, :, HD // 2 : HD // 2 + 1] * correct, (width, HD))
    else:
        acc_ref[...] = jnp.zeros((width, 2 * HD), F32)
    top_wide = jnp.broadcast_to(top, (width, 2 * BLK))
    ones = jnp.ones((2 * BLK, HD), BF16)

    def pair_sums(index, carry):
        weight = jnp.exp2(score_ref[index] * to_log2 - top_wide).astype(BF16)
        values = jnp.concatenate([kept_v[pl.ds(index * 2, 2)].reshape(2 * BLK, HD), ones], axis=1)
        acc_ref[...] += jnp.dot(weight, values, preferred_element_type=F32)
        return carry

    lax.fori_loop(0, lax.div(count + 1, 2), pair_sums, 0)
    if last:
        heads = acc_ref[:, :HD] / acc_ref[:, HD:]
        for g in range(group_size):
            out_ref[0, :, g * HD : (g + 1) * HD] = heads[g * q_rows : (g + 1) * q_rows].astype(BF16)
    else:
        acc_out[0] = acc_ref[:, :HD]
        lane = lax.broadcasted_iota(jnp.int32, (width, HD), 1)
        stat_out[0] = jnp.where(lane < HD // 2, jnp.broadcast_to(top, (width, HD)), acc_ref[:, HD:])


def attend(where, ranges, position, q, key_list, value_list, state, last, group_size, per_device):
    pieces, q_rows, features = q.shape
    sources = len(key_list)
    blocks = key_list[0].shape[0]
    width = q_rows * group_size
    nr = ranges.shape[0] // (2 * STRETCHES)
    first = state is None
    most = sources * blocks
    spec = (sources, blocks // per_device, per_device, group_size, first, last, nr)
    row = lambda shape: pl.BlockSpec((1,) + shape, lambda i: (i, 0, 0))
    state_specs = [row((width, HD)), row((width, HD))]
    state_shapes = [jax.ShapeDtypeStruct((pieces, width, HD), F32)] * 2
    return pl.pallas_call(
        functools.partial(attend_kernel, spec),
        grid=(pieces,),
        in_specs=[SMEM] * 3 + [row((q_rows, features))] + [VMEM] * (2 * sources) + ([] if first else state_specs),
        out_specs=row((q_rows, features)) if last else state_specs,
        out_shape=jax.ShapeDtypeStruct(q.shape, BF16) if last else state_shapes,
        scratch_shapes=[
            pltpu.VMEM((most + 2, BLK, HD), BF16),
            pltpu.VMEM((most + 2, BLK, HD), BF16),
            pltpu.VMEM((most // 2 + 1, width, 2 * BLK), F32),
            pltpu.VMEM((width, 2 * HD), F32),
            pltpu.SMEM((1,), jnp.int32),
        ],
        compiler_params=pltpu.CompilerParams(vmem_limit_bytes=ROOM),
    )(where, ranges, position, q, *key_list, *value_list, *(() if first else state))


def pieces_kernel(split, where_ref, *refs):
    inputs = len(refs) // (split + 1)
    for index in range(inputs):
        source = refs[index]
        width = source.shape[1] // split
        for step in range(split):
            start = pl.multiple_of(jnp.bitwise_xor(where_ref[0], step) * width, HD)
            refs[inputs + index * split + step][...] = source[:, pl.ds(start, width)]


def pieces_of(where, split, *arrays):
    shapes = []
    for array in arrays:
        shapes += [jax.ShapeDtypeStruct((array.shape[0], array.shape[1] // split), array.dtype)] * split
    out = pl.pallas_call(
        functools.partial(pieces_kernel, split),
        in_specs=[SMEM] + [VMEM] * len(arrays),
        out_specs=[VMEM] * len(shapes),
        out_shape=shapes,
        compiler_params=pltpu.CompilerParams(vmem_limit_bytes=ROOM),
    )(where, *arrays)
    return [out[i * split : (i + 1) * split] for i in range(len(arrays))]


def square_kernel(*refs):
    total = None
    for ref in refs[:-1]:
        heads = ref[...].astype(F32)
        part = jnp.sum(heads * heads, axis=1, keepdims=True)
        total = part if total is None else total + part
    refs[-1][...] = jnp.broadcast_to(total, refs[-1].shape)


def finish_kernel(split, where_ref, noise_ref, square_ref, gain_ref, *refs):
    out_ref = refs[split]
    level = noise_ref[where_ref[1]]
    scale = 1.0 / jnp.sqrt(square_ref[:, :1] / D + 1e-06)
    width = refs[0].shape[1]
    for step in range(split):
        start = pl.multiple_of(jnp.bitwise_xor(where_ref[0], step) * width, HD)
        gain = gain_ref[pl.ds(level, 1), pl.ds(start, width)]
        out_ref[:, pl.ds(start, width)] = (refs[step][...].astype(F32) * scale * gain).astype(BF16)


def body(queries, keys, values, ranges, noise_ids, block_position, level_gain):
    devices = lax.axis_size("ctx")
    q_rows = queries.shape[0]
    heads_here = keys.shape[1] // HD
    group_size = queries.shape[1] // keys.shape[1]
    per_device = keys.shape[0] // BLK
    stretch_devices = devices // STRETCHES
    whole_groups = heads_here == stretch_devices and heads_here & (heads_here - 1) == 0
    split = heads_here if whole_groups else 1
    groups = devices // split
    me = lax.axis_index("ctx")
    place, group = lax.rem(me, split), lax.div(me, split)
    stretch = lax.div(me, stretch_devices)
    ranges_flat = ranges.reshape(-1)

    def where(sources):
        return jnp.stack([jnp.int32(x) if isinstance(x, int) else x for x in (place, stretch, *sources)]).astype(jnp.int32)

    def permute(array, pairs):
        return lax.ppermute(array, "ctx", pairs)

    def within(step):
        return [(i, i ^ step) for i in range(devices)]

    def shift(step):
        return [(i, i + step * split) for i in range(devices) if 0 <= i + step * split < devices]

    here = where([group])
    if whole_groups:
        key_pieces, value_pieces = pieces_of(here, split, keys, values)
        (query_pieces,) = pieces_of(here, split, queries)
        own = []
        for pieces in (key_pieces, value_pieces):
            got = [pieces[0]] + [permute(pieces[step], within(step)) for step in range(1, split)]
            own.append(jnp.concatenate(got, axis=0).reshape(split * per_device, BLK, HD))
        q = [query_pieces[0]] + [permute(query_pieces[step], within(step)) for step in range(1, split)]
        q = jnp.stack(q)
        phases = []
        down, up = list(own), list(own)
        for step in range(1, groups):
            for which in range(2):
                down[which] = permute(down[which], shift(-1))
                up[which] = permute(up[which], shift(1))
            after = jnp.where(group + step < groups, group + step, -1)
            before = jnp.where(group - step >= 0, group - step, -1)
            phases.append(([down[0], up[0]], [down[1], up[1]], [after, before]))
        first_keys, first_values, first_groups = phases[0]
        phases[0] = ([own[0]] + first_keys, [own[1]] + first_values, [group] + first_groups)
        state = None
        for index, (key_list, value_list, sources) in enumerate(phases):
            state = attend(
                where(sources), ranges_flat, block_position, q, key_list, value_list, state,
                index == len(phases) - 1, group_size, per_device,
            )
        heads = state
        outs = [heads[0]] + [permute(heads[step], within(step)) for step in range(1, split)]
    else:
        key_all = lax.all_gather(keys, "ctx", axis=0, tiled=True)
        value_all = lax.all_gather(values, "ctx", axis=0, tiled=True)
        chunk = min(32, key_all.shape[0] // BLK)
        outs = []
        for head in range(heads_here):
            columns = slice(head * HD, (head + 1) * HD)
            q = queries[None, :, head * group_size * HD : (head + 1) * group_size * HD]
            head_keys = key_all[:, columns].reshape(-1, chunk, BLK, HD)
            head_values = value_all[:, columns].reshape(-1, chunk, BLK, HD)
            state, chunks = None, head_keys.shape[0]
            for index in range(chunks):
                numbers = jnp.stack([jnp.int32(0), stretch, jnp.int32(index)])
                state = attend(
                    numbers, ranges_flat, block_position, q, [head_keys[index]], [head_values[index]], state,
                    index == chunks - 1, group_size, chunk,
                )
            outs.append(state[0])
        outs = [jnp.concatenate(outs, axis=1)]
    square = pl.pallas_call(
        square_kernel,
        in_specs=[VMEM] * len(outs),
        out_specs=VMEM,
        out_shape=jax.ShapeDtypeStruct((q_rows, HD), F32),
    )(*outs)[:, 0]
    square = lax.psum(square, "head")
    return pl.pallas_call(
        functools.partial(finish_kernel, split),
        in_specs=[SMEM, SMEM] + [VMEM] * (2 + split),
        out_specs=VMEM,
        out_shape=jax.ShapeDtypeStruct(queries.shape, BF16),
        compiler_params=pltpu.CompilerParams(vmem_limit_bytes=ROOM),
    )(here, noise_ids, jnp.broadcast_to(square[:, None], (q_rows, HD)), level_gain, *outs)


def solution(mesh):
    placed = (P("ctx", "head"), P("ctx", "head"), P("ctx", "head"), P(), P(), P(), P(None, "head"))
    return jax.shard_map(
        body, mesh=mesh, in_specs=placed, out_specs=P("ctx", "head"), check_vma=False
    )
```

```python
import functools

import jax
import jax.numpy as jnp
from jax import lax
from jax.experimental import pallas as pl
from jax.experimental.pallas import tpu as pltpu
from jax.sharding import PartitionSpec as P

D = 6144
HD = 128
BLK = 128
STRETCHES = 4
LOG2E = 1.4426950408889634
NEGATIVE = -1e30

F32 = jnp.float32
BF16 = jnp.bfloat16
VMEM = pl.BlockSpec(memory_space=pltpu.VMEM)
SMEM = pl.BlockSpec(memory_space=pltpu.SMEM)
ROOM = 56 * 1024 * 1024


def attend_kernel(spec, *refs):
    sources, groups, split, per_device, pieces, group_size, first, last, nr = spec
    where_ref, ranges_ref, position_ref = refs[:3]
    at = 3
    query_refs = refs[at : at + pieces]
    at += pieces
    key_refs, value_refs = refs[at : at + len(sources)], refs[at + len(sources) : at + 2 * len(sources)]
    at += 2 * len(sources)
    if not first:
        acc_in, stat_in = refs[at : at + 2]
        at += 2
    if last:
        out_refs, square_refs = refs[at : at + pieces], refs[at + pieces : at + 2 * pieces]
        at += 2 * pieces
    else:
        acc_out, stat_out = refs[at : at + 2]
        at += 2
    kept_k, kept_v, score_ref, acc_ref = refs[at : at + 4]
    q_rows = query_refs[0].shape[0]
    width = pieces * q_rows * group_size
    to_log2 = LOG2E / HD**0.5

    place, stretch, group = where_ref[0], where_ref[1], where_ref[2]
    odd = lax.rem(group, 2) == 1
    count = jnp.int32(0)
    for index, (forward, distance) in enumerate(sources):
        held = jnp.where(odd, group - distance, group + distance) if forward else jnp.where(odd, group + distance, group - distance)
        inside = (held >= 0) & (held < groups)
        held = jnp.clip(held, 0, groups - 1)
        for step in range(split):
            device = held * split + jnp.bitwise_xor(place, step)
            for block in range(per_device):
                logical = position_ref[device * per_device + block]
                live = jnp.bool_(False)
                for r in range(nr):
                    low = ranges_ref[(stretch * nr + r) * 2]
                    high = ranges_ref[(stretch * nr + r) * 2 + 1]
                    live = live | ((logical >= low) & (logical < high))
                live = live & inside

                @pl.when(live)
                def _(count=count, index=index, slot=step * per_device + block):
                    kept_k[count] = key_refs[index][slot]
                    kept_v[count] = value_refs[index][slot]

                count = count + live.astype(jnp.int32)
    kept_v[count] = jnp.zeros((BLK, HD), BF16)

    pairs = lax.div(count, 2)
    quads = lax.div(count, 4)
    q = jnp.concatenate(
        [ref[:, g * HD : (g + 1) * HD] for ref in query_refs for g in range(group_size)], axis=0
    )
    acc_ref[:, :HD] = jnp.full((width, HD), NEGATIVE, F32)

    def scores(start, blocks):
        keys = kept_k[pl.ds(start, blocks)].reshape(blocks * BLK, HD)
        score = lax.dot_general(q, keys, (((1,), (1,)), ((), ())), preferred_element_type=F32)
        top = score[:, :BLK]
        for b in range(1, blocks):
            top = jnp.maximum(top, score[:, b * BLK : (b + 1) * BLK])
        acc_ref[:, :HD] = jnp.maximum(acc_ref[:, :HD], top)
        return score

    def quad_scores(index, carry):
        score = scores(index * 4, 4)
        score_ref[index * 2] = score[:, : 2 * BLK]
        score_ref[index * 2 + 1] = score[:, 2 * BLK :]
        return carry

    def pair_scores(index, carry):
        score_ref[index] = scores(index * 2, 2)
        return carry

    lax.fori_loop(0, quads, quad_scores, 0)
    lax.fori_loop(quads * 2, pairs, pair_scores, 0)

    @pl.when(count > pairs * 2)
    def _():
        score_ref[pairs, :, :BLK] = scores(count - 1, 1)
        score_ref[pairs, :, BLK:] = jnp.full((width, BLK), NEGATIVE, F32)

    top = jnp.max(acc_ref[:, :HD], axis=1, keepdims=True) * to_log2
    if not first:
        old_top = stat_in[:, :1]
        top = jnp.maximum(top, old_top)
        correct = jnp.exp2(old_top - top)
        acc_ref[:, :HD] = acc_in[...] * correct
        acc_ref[:, HD:] = jnp.broadcast_to(stat_in[:, HD // 2 : HD // 2 + 1] * correct, (width, HD))
    else:
        acc_ref[...] = jnp.zeros((width, 2 * HD), F32)
    top_wide = jnp.broadcast_to(top, (width, 2 * BLK))
    ones = jnp.ones((2 * BLK, HD), BF16)

    def sums(index):
        weight = jnp.exp2(score_ref[index] * to_log2 - top_wide).astype(BF16)
        values = jnp.concatenate([kept_v[pl.ds(index * 2, 2)].reshape(2 * BLK, HD), ones], axis=1)
        return jnp.dot(weight, values, preferred_element_type=F32)

    def quad_sums(index, carry):
        acc_ref[...] += sums(index * 2) + sums(index * 2 + 1)
        return carry

    def pair_sums(index, carry):
        acc_ref[...] += sums(index)
        return carry

    steps = lax.div(count + 1, 2)
    twice = lax.div(steps, 2)
    lax.fori_loop(0, twice, quad_sums, 0)
    lax.fori_loop(twice * 2, steps, pair_sums, 0)
    if last:
        heads = acc_ref[:, :HD] / acc_ref[:, HD:]
        for p in range(pieces):
            square = jnp.zeros((q_rows, 1), F32)
            for g in range(group_size):
                start = (p * group_size + g) * q_rows
                part = heads[start : start + q_rows]
                square = square + jnp.sum(part * part, axis=1, keepdims=True)
                out_refs[p][:, g * HD : (g + 1) * HD] = part.astype(BF16)
            square_refs[p][...] = jnp.broadcast_to(square, (q_rows, q_rows)).T[:8]
    else:
        acc_out[...] = acc_ref[:, :HD]
        lane = lax.broadcasted_iota(jnp.int32, (width, HD), 1)
        stat_out[...] = jnp.where(lane < HD // 2, jnp.broadcast_to(top, (width, HD)), acc_ref[:, HD:])


def attend(where, ranges, position, q, key_list, value_list, sources, groups, state, last, group_size, per_device):
    pieces = len(q)
    q_rows = q[0].shape[0]
    blocks = key_list[0].shape[0]
    width = pieces * q_rows * group_size
    nr = ranges.shape[0] // (2 * STRETCHES)
    first = state is None
    most = len(sources) * blocks
    spec = (sources, groups, blocks // per_device, per_device, pieces, group_size, first, last, nr)
    if last:
        shapes = [jax.ShapeDtypeStruct(q[0].shape, BF16)] * pieces + [jax.ShapeDtypeStruct((8, q_rows), F32)] * pieces
    else:
        shapes = [jax.ShapeDtypeStruct((width, HD), F32)] * 2
    inputs = 2 * len(sources) + pieces + (0 if first else 2)
    return pl.pallas_call(
        functools.partial(attend_kernel, spec),
        in_specs=[SMEM] * 3 + [VMEM] * inputs,
        out_specs=[VMEM] * len(shapes),
        out_shape=shapes,
        scratch_shapes=[
            pltpu.VMEM((most + 2, BLK, HD), BF16),
            pltpu.VMEM((most + 2, BLK, HD), BF16),
            pltpu.VMEM((most // 2 + 1, width, 2 * BLK), F32),
            pltpu.VMEM((width, 2 * HD), F32),
        ],
        compiler_params=pltpu.CompilerParams(vmem_limit_bytes=ROOM),
        cost_estimate=pl.CostEstimate(
            flops=12 * width * most * BLK * HD, bytes_accessed=4 * width * HD, transcendentals=width * most * BLK
        ),
    )(where, ranges, position, *q, *key_list, *value_list, *(() if first else state))


def pieces_kernel(split, where_ref, *refs):
    inputs = len(refs) // (split + 1)
    for index in range(inputs):
        source = refs[index]
        width = source.shape[1] // split
        for step in range(split):
            start = pl.multiple_of(jnp.bitwise_xor(where_ref[0], step) * width, HD)
            refs[inputs + index * split + step][...] = source[:, pl.ds(start, width)]


def pieces_of(where, split, *arrays):
    shapes = []
    for array in arrays:
        shapes += [jax.ShapeDtypeStruct((array.shape[0], array.shape[1] // split), array.dtype)] * split
    out = pl.pallas_call(
        functools.partial(pieces_kernel, split),
        in_specs=[SMEM] + [VMEM] * len(arrays),
        out_specs=[VMEM] * len(shapes),
        out_shape=shapes,
        compiler_params=pltpu.CompilerParams(vmem_limit_bytes=ROOM),
    )(where, *arrays)
    return [out[i * split : (i + 1) * split] for i in range(len(arrays))]


def finish_kernel(split, where_ref, noise_ref, square_ref, gain_ref, *refs):
    out_ref = refs[split]
    q_rows, width = refs[0].shape
    level = noise_ref[where_ref[1]]
    square = jnp.broadcast_to(square_ref[:1], (q_rows, q_rows)).T[:, :1]
    scale = 1.0 / jnp.sqrt(square / D + 1e-06)
    for step in range(split):
        start = pl.multiple_of(jnp.bitwise_xor(where_ref[0], step) * width, HD)
        gain = gain_ref[pl.ds(level, 1), pl.ds(start, width)]
        out_ref[:, pl.ds(start, width)] = (refs[step][...].astype(F32) * scale * gain).astype(BF16)


def body(queries, keys, values, ranges, noise_ids, block_position, level_gain):
    devices = lax.axis_size("ctx")
    q_rows = queries.shape[0]
    heads_here = keys.shape[1] // HD
    group_size = queries.shape[1] // keys.shape[1]
    per_device = keys.shape[0] // BLK
    stretch_devices = devices // STRETCHES
    shared = heads_here == stretch_devices and heads_here & (heads_here - 1) == 0 and STRETCHES % 2 == 0
    split = heads_here if shared else 1
    groups = devices // split
    me = lax.axis_index("ctx")
    here = jnp.stack([lax.rem(me, split), lax.div(me, stretch_devices), lax.div(me, split)]).astype(jnp.int32)
    ranges_flat = ranges.reshape(-1)

    def permute(array, pairs):
        return lax.ppermute(array, "ctx", pairs)

    def within(step):
        return [(i, i ^ step) for i in range(devices)]

    def between(offset):
        pairs = []
        for i in range(devices):
            other = i // split + (1 if i // split % 2 == offset else -1)
            pairs.append((i, other * split + i % split if 0 <= other < groups else i))
        return pairs

    if shared:
        key_pieces, value_pieces = pieces_of(here, split, keys, values)
        (query_pieces,) = pieces_of(here, split, queries)
        own = []
        for pieces in (key_pieces, value_pieces):
            got = [pieces[0]] + [permute(pieces[step], within(step)) for step in range(1, split)]
            own.append(jnp.concatenate(got, axis=0).reshape(split * per_device, BLK, HD))
        q = [query_pieces[0]] + [permute(query_pieces[step], within(step)) for step in range(1, split)]
        phases = [([own[0]], [own[1]], ((True, 0),))]
        even, odd = list(own), list(own)
        for step in range(1, groups):
            ends = step == groups - 1
            for which in range(2):
                even[which], odd[which] = permute(odd[which], between(0)), (
                    None if ends else permute(even[which], between(1))
                )
            if ends:
                phases.append(([even[0]], [even[1]], ((True, step),)))
            else:
                phases.append(([even[0], odd[0]], [even[1], odd[1]], ((True, step), (False, step))))
        state = None
        for index, (key_list, value_list, sources) in enumerate(phases):
            state = attend(
                here, ranges_flat, block_position, q, key_list, value_list, sources, groups, state,
                index == len(phases) - 1, group_size, per_device,
            )
        outs, squares = state[:split], state[split:]
        square = squares[0]
        for step in range(1, split):
            square = square + permute(squares[step], within(step))
        outs = [outs[0]] + [permute(outs[step], within(step)) for step in range(1, split)]
    else:
        key_all = lax.all_gather(keys, "ctx", axis=0, tiled=True)
        value_all = lax.all_gather(values, "ctx", axis=0, tiled=True)
        chunk = min(32, key_all.shape[0] // BLK)
        outs, square = [], 0.0
        for head in range(heads_here):
            columns = slice(head * HD, (head + 1) * HD)
            q = [queries[:, head * group_size * HD : (head + 1) * group_size * HD]]
            head_keys = key_all[:, columns].reshape(-1, chunk, BLK, HD)
            head_values = value_all[:, columns].reshape(-1, chunk, BLK, HD)
            state, chunks = None, head_keys.shape[0]
            for index in range(chunks):
                numbers = jnp.stack([jnp.int32(0), here[1], jnp.int32(0)])
                state = attend(
                    numbers, ranges_flat, block_position, q, [head_keys[index]], [head_values[index]],
                    ((True, index),), chunks, state, index == chunks - 1, group_size, chunk,
                )
            outs.append(state[0])
            square = square + state[1]
        outs = [jnp.concatenate(outs, axis=1)]
    square = lax.psum(square, "head")
    return pl.pallas_call(
        functools.partial(finish_kernel, split),
        in_specs=[SMEM, SMEM] + [VMEM] * (2 + split),
        out_specs=VMEM,
        out_shape=jax.ShapeDtypeStruct(queries.shape, BF16),
        compiler_params=pltpu.CompilerParams(vmem_limit_bytes=ROOM),
    )(here, noise_ids, square, level_gain, *outs)


def solution(mesh):
    placed = (P("ctx", "head"), P("ctx", "head"), P("ctx", "head"), P(), P(), P(), P(None, "head"))
    return jax.shard_map(
        body, mesh=mesh, in_specs=placed, out_specs=P("ctx", "head"), check_vma=False
    )
```

```python
import functools

import jax
import jax.numpy as jnp
from jax import lax
from jax.experimental import pallas as pl
from jax.experimental.pallas import tpu as pltpu
from jax.sharding import PartitionSpec as P

D = 6144
HD = 128
BLK = 128
STRETCHES = 4
LOG2E = 1.4426950408889634
NEGATIVE = -1e30

F32 = jnp.float32
BF16 = jnp.bfloat16
VMEM = pl.BlockSpec(memory_space=pltpu.VMEM)
SMEM = pl.BlockSpec(memory_space=pltpu.SMEM)
ROOM = 52 * 1024 * 1024


def attend_kernel(spec, *refs):
    sources, split, per_device, pieces, group_size, first, last, nr = spec
    where_ref, ranges_ref, position_ref = refs[:3]
    at = 3
    query_refs = refs[at : at + pieces]
    at += pieces
    key_refs, value_refs = refs[at : at + len(sources)], refs[at + len(sources) : at + 2 * len(sources)]
    at += 2 * len(sources)
    if not first:
        acc_in, stat_in = refs[at : at + 2]
        at += 2
    if last:
        out_refs, square_refs = refs[at : at + pieces], refs[at + pieces : at + 2 * pieces]
        at += 2 * pieces
    else:
        acc_out, stat_out = refs[at : at + 2]
        at += 2
    kept_k, kept_v, score_ref, acc_ref = refs[at : at + 4]
    at += 4
    if not first:
        acc_old, stat_old, semaphores = refs[at : at + 3]
        fetches = [
            pltpu.make_async_copy(acc_in, acc_old, semaphores.at[0]),
            pltpu.make_async_copy(stat_in, stat_old, semaphores.at[1]),
        ]
        for fetch in fetches:
            fetch.start()
    q_rows = query_refs[0].shape[0]
    width = pieces * q_rows * group_size
    to_log2 = LOG2E / HD**0.5

    place, stretch, group = where_ref[0], where_ref[1], where_ref[2]
    count = jnp.int32(0)
    for index, bits in enumerate(sources):
        held = jnp.bitwise_xor(group, bits)
        for step in range(split):
            device = held * split + jnp.bitwise_xor(place, step)
            for block in range(per_device):
                logical = position_ref[device * per_device + block]
                live = jnp.bool_(False)
                for r in range(nr):
                    low = ranges_ref[(stretch * nr + r) * 2]
                    high = ranges_ref[(stretch * nr + r) * 2 + 1]
                    live = live | ((logical >= low) & (logical < high))

                @pl.when(live)
                def _(count=count, index=index, slot=step * per_device + block):
                    kept_k[count] = key_refs[index][slot]
                    kept_v[count] = value_refs[index][slot]

                count = count + live.astype(jnp.int32)
    kept_v[count] = jnp.zeros((BLK, HD), BF16)

    pairs = lax.div(count, 2)
    quads = lax.div(count, 4)
    q = jnp.concatenate(
        [ref[:, g * HD : (g + 1) * HD] for ref in query_refs for g in range(group_size)], axis=0
    )
    acc_ref[:, :HD] = jnp.full((width, HD), NEGATIVE, F32)

    def scores(start, blocks):
        keys = kept_k[pl.ds(start, blocks)].reshape(blocks * BLK, HD)
        score = lax.dot_general(q, keys, (((1,), (1,)), ((), ())), preferred_element_type=F32)
        top = score[:, :BLK]
        for b in range(1, blocks):
            top = jnp.maximum(top, score[:, b * BLK : (b + 1) * BLK])
        acc_ref[:, :HD] = jnp.maximum(acc_ref[:, :HD], top)
        return score

    def quad_scores(index, carry):
        score = scores(index * 4, 4)
        score_ref[index * 2] = score[:, : 2 * BLK]
        score_ref[index * 2 + 1] = score[:, 2 * BLK :]
        return carry

    def pair_scores(index, carry):
        score_ref[index] = scores(index * 2, 2)
        return carry

    lax.fori_loop(0, quads, quad_scores, 0)
    lax.fori_loop(quads * 2, pairs, pair_scores, 0)

    @pl.when(count > pairs * 2)
    def _():
        score_ref[pairs, :, :BLK] = scores(count - 1, 1)
        score_ref[pairs, :, BLK:] = jnp.full((width, BLK), NEGATIVE, F32)

    top = jnp.max(acc_ref[:, :HD], axis=1, keepdims=True) * to_log2
    if not first:
        for fetch in fetches:
            fetch.wait()
        old_top = stat_old[:, :1]
        top = jnp.maximum(top, old_top)
        correct = jnp.exp2(old_top - top)
        acc_ref[:, :HD] = acc_old[...] * correct
        acc_ref[:, HD:] = jnp.broadcast_to(stat_old[:, HD // 2 : HD // 2 + 1] * correct, (width, HD))
    else:
        acc_ref[...] = jnp.zeros((width, 2 * HD), F32)
    top_wide = jnp.broadcast_to(top, (width, 2 * BLK))
    ones = jnp.ones((2 * BLK, HD), BF16)

    def sums(index):
        weight = jnp.exp2(score_ref[index] * to_log2 - top_wide).astype(BF16)
        values = jnp.concatenate([kept_v[pl.ds(index * 2, 2)].reshape(2 * BLK, HD), ones], axis=1)
        return jnp.dot(weight, values, preferred_element_type=F32)

    def quad_sums(index, carry):
        acc_ref[...] += sums(index * 2) + sums(index * 2 + 1)
        return carry

    def pair_sums(index, carry):
        acc_ref[...] += sums(index)
        return carry

    steps = lax.div(count + 1, 2)
    twice = lax.div(steps, 2)
    lax.fori_loop(0, twice, quad_sums, 0)
    lax.fori_loop(twice * 2, steps, pair_sums, 0)
    if last:
        heads = acc_ref[:, :HD] / acc_ref[:, HD:]
        for p in range(pieces):
            square = jnp.zeros((q_rows, HD), F32)
            for g in range(group_size):
                start = (p * group_size + g) * q_rows
                part = heads[start : start + q_rows]
                square = square + part * part
                out_refs[p][:, g * HD : (g + 1) * HD] = part.astype(BF16)
            square = jnp.sum(square, axis=1, keepdims=True)
            square_refs[p][...] = jnp.broadcast_to(square, (q_rows, q_rows)).T[:8]
    else:
        acc_out[...] = acc_ref[:, :HD]
        lane = lax.broadcasted_iota(jnp.int32, (width, HD), 1)
        stat_out[...] = jnp.where(lane < HD // 2, jnp.broadcast_to(top, (width, HD)), acc_ref[:, HD:])


def attend(where, ranges, position, q, key_list, value_list, sources, state, last, group_size, per_device):
    pieces = len(q)
    q_rows = q[0].shape[0]
    blocks = key_list[0].shape[0]
    width = pieces * q_rows * group_size
    nr = ranges.shape[0] // (2 * STRETCHES)
    first = state is None
    most = len(sources) * blocks
    spec = (tuple(sources), blocks // per_device, per_device, pieces, group_size, first, last, nr)
    if last:
        shapes = [jax.ShapeDtypeStruct(q[0].shape, BF16)] * pieces + [jax.ShapeDtypeStruct((8, q_rows), F32)] * pieces
    else:
        shapes = [jax.ShapeDtypeStruct((width, HD), F32)] * 2
    inputs = 2 * len(sources) + pieces
    held = [] if first else [pltpu.VMEM((width, HD), F32)] * 2 + [pltpu.SemaphoreType.DMA((2,))]
    return pl.pallas_call(
        functools.partial(attend_kernel, spec),
        in_specs=[SMEM] * 3 + [VMEM] * inputs + [pl.BlockSpec(memory_space=pl.ANY)] * (0 if first else 2),
        out_specs=[VMEM] * len(shapes),
        out_shape=shapes,
        scratch_shapes=[
            pltpu.VMEM((most + 2, BLK, HD), BF16),
            pltpu.VMEM((most + 2, BLK, HD), BF16),
            pltpu.VMEM((most // 2 + 1, width, 2 * BLK), F32),
            pltpu.VMEM((width, 2 * HD), F32),
            *held,
        ],
        compiler_params=pltpu.CompilerParams(vmem_limit_bytes=ROOM),
        cost_estimate=pl.CostEstimate(
            flops=12 * width * most * BLK * HD, bytes_accessed=4 * width * HD, transcendentals=width * most * BLK
        ),
    )(where, ranges, position, *q, *key_list, *value_list, *(() if first else state))


def pieces_kernel(split, where_ref, *refs):
    inputs = len(refs) // (split + 1)
    for index in range(inputs):
        source = refs[index]
        width = source.shape[1] // split
        for step in range(split):
            start = pl.multiple_of(jnp.bitwise_xor(where_ref[0], step) * width, HD)
            refs[inputs + index * split + step][...] = source[:, pl.ds(start, width)]


def pieces_of(where, split, *arrays):
    shapes = []
    for array in arrays:
        shapes += [jax.ShapeDtypeStruct((array.shape[0], array.shape[1] // split), array.dtype)] * split
    out = pl.pallas_call(
        functools.partial(pieces_kernel, split),
        in_specs=[SMEM] + [VMEM] * len(arrays),
        out_specs=[VMEM] * len(shapes),
        out_shape=shapes,
    )(where, *arrays)
    return [out[i * split : (i + 1) * split] for i in range(len(arrays))]


def finish_kernel(split, where_ref, noise_ref, square_ref, gain_ref, *refs):
    out_ref = refs[split]
    q_rows, width = refs[0].shape
    level = noise_ref[where_ref[1]]
    square = jnp.broadcast_to(square_ref[:1], (q_rows, q_rows)).T[:, :1]
    scale = 1.0 / jnp.sqrt(square / D + 1e-06)
    for step in range(split):
        start = pl.multiple_of(jnp.bitwise_xor(where_ref[0], step) * width, HD)
        gain = gain_ref[pl.ds(level, 1), pl.ds(start, width)]
        out_ref[:, pl.ds(start, width)] = (refs[step][...].astype(F32) * scale * gain).astype(BF16)


def body(queries, keys, values, ranges, noise_ids, block_position, level_gain):
    devices = lax.axis_size("ctx")
    q_rows = queries.shape[0]
    heads_here = keys.shape[1] // HD
    group_size = queries.shape[1] // keys.shape[1]
    per_device = keys.shape[0] // BLK
    stretch_devices = devices // STRETCHES
    shared = heads_here == stretch_devices and heads_here & (heads_here - 1) == 0 and STRETCHES & (STRETCHES - 1) == 0
    split = heads_here if shared else 1
    groups = devices // split
    me = lax.axis_index("ctx")
    here = jnp.stack([lax.rem(me, split), lax.div(me, stretch_devices), lax.div(me, split)]).astype(jnp.int32)
    ranges_flat = ranges.reshape(-1)

    def permute(array, pairs):
        return lax.ppermute(array, "ctx", pairs)

    def within(step):
        return [(i, i ^ step) for i in range(devices)]

    def between(bits):
        return [(i, (i // split ^ bits) * split + i % split) for i in range(devices)]

    if shared:
        key_pieces, value_pieces = pieces_of(here, split, keys, values)
        (query_pieces,) = pieces_of(here, split, queries)
        own = []
        for pieces in (key_pieces, value_pieces):
            got = [pieces[0]] + [permute(pieces[step], within(step)) for step in range(1, split)]
            own.append(jnp.concatenate(got, axis=0).reshape(split * per_device, BLK, HD))
        q = [query_pieces[0]] + [permute(query_pieces[step], within(step)) for step in range(1, split)]
        have = [(0, own)]
        reach = groups
        while reach > 1:
            have += [(bits ^ (reach - 1), [permute(array, between(reach - 1)) for array in rows]) for bits, rows in have]
            reach //= 2
        phases = [have[:1], have[1:-1], have[-1:]]
        state = None
        for index, phase in enumerate(phases):
            state = attend(
                here, ranges_flat, block_position, q, [rows[0] for _, rows in phase], [rows[1] for _, rows in phase],
                [bits for bits, _ in phase], state, index == len(phases) - 1, group_size, per_device,
            )
        outs, squares = state[:split], state[split:]
        square = squares[0]
        for step in range(1, split):
            square = square + permute(squares[step], within(step))
        outs = [outs[0]] + [permute(outs[step], within(step)) for step in range(1, split)]
    else:
        key_all = lax.all_gather(keys, "ctx", axis=0, tiled=True)
        value_all = lax.all_gather(values, "ctx", axis=0, tiled=True)
        chunk = min(32, key_all.shape[0] // BLK)
        outs, square = [], 0.0
        for head in range(heads_here):
            columns = slice(head * HD, (head + 1) * HD)
            q = [queries[:, head * group_size * HD : (head + 1) * group_size * HD]]
            head_keys = key_all[:, columns].reshape(-1, chunk, BLK, HD)
            head_values = value_all[:, columns].reshape(-1, chunk, BLK, HD)
            state, chunks = None, head_keys.shape[0]
            for index in range(chunks):
                numbers = jnp.stack([jnp.int32(0), here[1], jnp.int32(0)])
                state = attend(
                    numbers, ranges_flat, block_position, q, [head_keys[index]], [head_values[index]],
                    [index], state, index == chunks - 1, group_size, chunk,
                )
            outs.append(state[0])
            square = square + state[1]
        outs = [jnp.concatenate(outs, axis=1)]
    square = lax.psum(square, "head")
    return pl.pallas_call(
        functools.partial(finish_kernel, split),
        in_specs=[SMEM, SMEM] + [VMEM] * (2 + split),
        out_specs=VMEM,
        out_shape=jax.ShapeDtypeStruct(queries.shape, BF16),
    )(here, noise_ids, square, level_gain, *outs)


def solution(mesh):
    placed = (P("ctx", "head"), P("ctx", "head"), P("ctx", "head"), P(), P(), P(), P(None, "head"))
    return jax.shard_map(
        body, mesh=mesh, in_specs=placed, out_specs=P("ctx", "head"), check_vma=False
    )
```

```python
import functools

import jax
import jax.numpy as jnp
from jax import lax
from jax.experimental import pallas as pl
from jax.experimental.pallas import tpu as pltpu
from jax.sharding import PartitionSpec as P

D = 6144
HD = 128
BLK = 128
STRETCHES = 4
LOG2E = 1.4426950408889634
NEGATIVE = -1e30

F32 = jnp.float32
BF16 = jnp.bfloat16
VMEM = pl.BlockSpec(memory_space=pltpu.VMEM)
SMEM = pl.BlockSpec(memory_space=pltpu.SMEM)
ROOM = 52 * 1024 * 1024


def attend_kernel(spec, *refs):
    sources, split, per_device, pieces, group_size, first, last, nr = spec
    where_ref, ranges_ref, position_ref = refs[:3]
    at = 3
    query_refs = refs[at : at + pieces]
    at += pieces
    row_refs = refs[at : at + len(sources)]
    at += len(sources)
    if not first:
        acc_in, stat_in = refs[at : at + 2]
        at += 2
    if last:
        out_refs, square_refs = refs[at : at + pieces], refs[at + pieces : at + 2 * pieces]
        at += 2 * pieces
    else:
        acc_out, stat_out = refs[at : at + 2]
        at += 2
    kept_k, kept_v, score_ref, acc_ref = refs[at : at + 4]
    at += 4
    if not first:
        acc_old, stat_old, semaphores = refs[at : at + 3]
        fetches = [
            pltpu.make_async_copy(acc_in, acc_old, semaphores.at[0]),
            pltpu.make_async_copy(stat_in, stat_old, semaphores.at[1]),
        ]
        for fetch in fetches:
            fetch.start()
    q_rows = query_refs[0].shape[0]
    width = pieces * q_rows * group_size
    to_log2 = LOG2E / HD**0.5

    place, stretch, group = where_ref[0], where_ref[1], where_ref[2]
    count = jnp.int32(0)
    for index, (bits, steps) in enumerate(sources):
        held = jnp.bitwise_xor(group, bits)
        for at_step, step in enumerate(steps):
            device = held * split + jnp.bitwise_xor(place, step)
            for block in range(per_device):
                logical = position_ref[device * per_device + block]
                live = jnp.bool_(False)
                for r in range(nr):
                    low, high = ranges_ref[r, 0, stretch], ranges_ref[r, 1, stretch]
                    live = live | ((logical >= low) & (logical < high))

                @pl.when(live)
                def _(count=count, index=index, slot=2 * at_step * per_device + block):
                    kept_k[count] = row_refs[index][slot]
                    kept_v[count] = row_refs[index][slot + per_device]

                count = count + live.astype(jnp.int32)
    kept_v[count] = jnp.zeros((BLK, HD), BF16)

    pairs = lax.div(count, 2)
    quads = lax.div(count, 4)
    q = jnp.concatenate(
        [ref[:, g * HD : (g + 1) * HD] for ref in query_refs for g in range(group_size)], axis=0
    )
    acc_ref[:, :HD] = jnp.full((width, HD), NEGATIVE, F32)

    def scores(start, blocks):
        keys = kept_k[pl.ds(start, blocks)].reshape(blocks * BLK, HD)
        score = lax.dot_general(q, keys, (((1,), (1,)), ((), ())), preferred_element_type=F32)
        top = score[:, :BLK]
        for b in range(1, blocks):
            top = jnp.maximum(top, score[:, b * BLK : (b + 1) * BLK])
        acc_ref[:, :HD] = jnp.maximum(acc_ref[:, :HD], top)
        return score

    def quad_scores(index, carry):
        score = scores(index * 4, 4)
        score_ref[index * 2] = score[:, : 2 * BLK]
        score_ref[index * 2 + 1] = score[:, 2 * BLK :]
        return carry

    def pair_scores(index, carry):
        score_ref[index] = scores(index * 2, 2)
        return carry

    lax.fori_loop(0, quads, quad_scores, 0)
    lax.fori_loop(quads * 2, pairs, pair_scores, 0)

    @pl.when(count > pairs * 2)
    def _():
        score_ref[pairs, :, :BLK] = scores(count - 1, 1)
        score_ref[pairs, :, BLK:] = jnp.full((width, BLK), NEGATIVE, F32)

    top = jnp.max(acc_ref[:, :HD], axis=1, keepdims=True) * to_log2
    if not first:
        for fetch in fetches:
            fetch.wait()
        old_top = stat_old[:, :1]
        top = jnp.maximum(top, old_top)
        correct = jnp.exp2(old_top - top)
        acc_ref[:, :HD] = acc_old[...] * correct
        acc_ref[:, HD:] = jnp.broadcast_to(stat_old[:, HD // 2 : HD // 2 + 1] * correct, (width, HD))
    else:
        acc_ref[...] = jnp.zeros((width, 2 * HD), F32)
    top_wide = jnp.broadcast_to(top, (width, 2 * BLK))
    ones = jnp.ones((2 * BLK, HD), BF16)

    def sums(index):
        weight = jnp.exp2(score_ref[index] * to_log2 - top_wide).astype(BF16)
        values = jnp.concatenate([kept_v[pl.ds(index * 2, 2)].reshape(2 * BLK, HD), ones], axis=1)
        return jnp.dot(weight, values, preferred_element_type=F32)

    def quad_sums(index, carry):
        acc_ref[...] += sums(index * 2) + sums(index * 2 + 1)
        return carry

    def pair_sums(index, carry):
        acc_ref[...] += sums(index)
        return carry

    steps = lax.div(count + 1, 2)
    twice = lax.div(steps, 2)
    lax.fori_loop(0, twice, quad_sums, 0)
    lax.fori_loop(twice * 2, steps, pair_sums, 0)
    if last:
        heads = acc_ref[:, :HD] / acc_ref[:, HD:]
        for p in range(pieces):
            square = jnp.zeros((q_rows, HD), F32)
            for g in range(group_size):
                start = (p * group_size + g) * q_rows
                part = heads[start : start + q_rows]
                square = square + part * part
                out_refs[p][:, g * HD : (g + 1) * HD] = part.astype(BF16)
            square = jnp.sum(square, axis=1, keepdims=True)
            square_refs[p][...] = jnp.broadcast_to(square, (q_rows, q_rows)).T[:8]
    else:
        acc_out[...] = acc_ref[:, :HD]
        lane = lax.broadcasted_iota(jnp.int32, (width, HD), 1)
        stat_out[...] = jnp.where(lane < HD // 2, jnp.broadcast_to(top, (width, HD)), acc_ref[:, HD:])


def attend(where, ranges, position, q, row_list, sources, state, last, group_size, split, per_device):
    pieces = len(q)
    q_rows = q[0].shape[0]
    width = pieces * q_rows * group_size
    nr = ranges.shape[0]
    first = state is None
    most = sum(rows.shape[0] for rows in row_list) // 2
    spec = (tuple(sources), split, per_device, pieces, group_size, first, last, nr)
    if last:
        shapes = [jax.ShapeDtypeStruct(q[0].shape, BF16)] * pieces + [jax.ShapeDtypeStruct((8, q_rows), F32)] * pieces
    else:
        shapes = [jax.ShapeDtypeStruct((width, HD), F32)] * 2
    inputs = len(sources) + pieces
    held = [] if first else [pltpu.VMEM((width, HD), F32)] * 2 + [pltpu.SemaphoreType.DMA((2,))]
    return pl.pallas_call(
        functools.partial(attend_kernel, spec),
        in_specs=[SMEM] * 3 + [VMEM] * inputs + [pl.BlockSpec(memory_space=pl.ANY)] * (0 if first else 2),
        out_specs=[VMEM] * len(shapes),
        out_shape=shapes,
        scratch_shapes=[
            pltpu.VMEM((most + 2, BLK, HD), BF16),
            pltpu.VMEM((most + 2, BLK, HD), BF16),
            pltpu.VMEM((most // 2 + 1, width, 2 * BLK), F32),
            pltpu.VMEM((width, 2 * HD), F32),
            *held,
        ],
        compiler_params=pltpu.CompilerParams(vmem_limit_bytes=ROOM),
        cost_estimate=pl.CostEstimate(
            flops=12 * width * most * BLK * HD, bytes_accessed=4 * width * HD, transcendentals=width * most * BLK
        ),
    )(where, ranges, position, *q, *row_list, *(() if first else state))


def pieces_kernel(split, inputs, where_ref, *refs):
    for step in range(split):
        row = 0
        for source in refs[:inputs]:
            rows, width = source.shape[0], source.shape[1] // split
            start = pl.multiple_of(jnp.bitwise_xor(where_ref[0], step) * width, HD)
            refs[len(refs) - split + step][row : row + rows] = source[:, pl.ds(start, width)]
            row += rows


def pieces_of(where, split, arrays, *before):
    rows = sum(array.shape[0] for array in arrays)
    shapes = [jax.ShapeDtypeStruct((rows, arrays[0].shape[1] // split), arrays[0].dtype)] * split
    return pl.pallas_call(
        functools.partial(pieces_kernel, split, len(arrays)),
        in_specs=[SMEM] + [VMEM] * len(arrays) + [pl.BlockSpec(memory_space=pl.ANY)] * len(before),
        out_specs=[VMEM] * split,
        out_shape=shapes,
    )(where, *arrays, *before)


def copy_kernel(rows_ref, before_ref, out_ref):
    out_ref[...] = rows_ref[...]


def copy_after(rows, before):
    return pl.pallas_call(
        copy_kernel,
        in_specs=[VMEM, pl.BlockSpec(memory_space=pl.ANY)],
        out_specs=VMEM,
        out_shape=jax.ShapeDtypeStruct(rows.shape, rows.dtype),
    )(rows, before)


def finish_kernel(split, where_ref, noise_ref, square_ref, gain_ref, *refs):
    out_ref = refs[split]
    q_rows, width = refs[0].shape
    level = noise_ref[where_ref[1]]
    square = jnp.broadcast_to(square_ref[:1], (q_rows, q_rows)).T[:, :1]
    scale = 1.0 / jnp.sqrt(square / D + 1e-06)
    for step in range(split):
        start = pl.multiple_of(jnp.bitwise_xor(where_ref[0], step) * width, HD)
        gain = gain_ref[pl.ds(level, 1), pl.ds(start, width)]
        out_ref[:, pl.ds(start, width)] = (refs[step][...].astype(F32) * scale * gain).astype(BF16)


def body(queries, keys, values, ranges, noise_ids, block_position, level_gain):
    devices = lax.axis_size("ctx")
    q_rows = queries.shape[0]
    heads_here = keys.shape[1] // HD
    group_size = queries.shape[1] // keys.shape[1]
    per_device = keys.shape[0] // BLK
    stretch_devices = devices // STRETCHES
    shared = heads_here == stretch_devices and heads_here & (heads_here - 1) == 0 and STRETCHES & (STRETCHES - 1) == 0
    split = heads_here if shared else 1
    groups = devices // split
    me = lax.axis_index("ctx")
    here = jnp.stack([lax.rem(me, split), lax.div(me, stretch_devices), lax.div(me, split)]).astype(jnp.int32)
    ranges_turned = ranges.transpose(1, 2, 0)

    def permute(array, pairs):
        return lax.ppermute(array, "ctx", pairs)

    def within(step):
        return [(i, i ^ step) for i in range(devices)]

    def between(bits):
        return [(i, (i // split ^ bits) * split + i % split) for i in range(devices)]

    if shared:
        row_pieces = pieces_of(here, split, [keys, values])
        query_pieces = pieces_of(here, split, [queries])
        got = [row_pieces[0]] + [permute(row_pieces[step], within(step)) for step in range(1, split)]
        halves = [range(split // 2), range(split // 2, split)]
        have = [
            (0, steps, jnp.concatenate([got[step] for step in steps], axis=0).reshape(-1, BLK, HD)) for steps in halves
        ]
        q = [query_pieces[0]] + [permute(query_pieces[step], within(step)) for step in range(1, split)]
        reach = groups
        while reach > 1:
            arrived = []
            for bits, steps, rows in have:
                if reach == groups and arrived:
                    rows = copy_after(rows, arrived[-1][2])
                arrived.append((bits ^ (reach - 1), steps, permute(rows, between(reach - 1))))
            have += arrived
            reach //= 2
        final = have[-1][0]
        phases = [
            [source for source in have if source[0] < 2],
            [source for source in have if source[0] >= 2 and source[0] != final],
            [source for source in have if source[0] == final],
        ]
        state = None
        for index, phase in enumerate(phases):
            state = attend(
                here, ranges_turned, block_position, q, [rows for _, _, rows in phase],
                [(bits, tuple(steps)) for bits, steps, _ in phase], state, index == len(phases) - 1,
                group_size, split, per_device,
            )
        outs, squares = state[:split], state[split:]
        square = squares[0]
        for step in range(1, split):
            square = square + permute(squares[step], within(step))
        outs = [outs[0]] + [permute(outs[step], within(step)) for step in range(1, split)]
    else:
        key_all = lax.all_gather(keys, "ctx", axis=0, tiled=True)
        value_all = lax.all_gather(values, "ctx", axis=0, tiled=True)
        chunk = min(32, key_all.shape[0] // BLK)
        outs, square = [], 0.0
        for head in range(heads_here):
            columns = slice(head * HD, (head + 1) * HD)
            q = [queries[:, head * group_size * HD : (head + 1) * group_size * HD]]
            rows = [array[:, columns].reshape(-1, chunk, BLK, HD) for array in (key_all, value_all)]
            rows = jnp.concatenate(rows, axis=1)
            state, chunks = None, rows.shape[0]
            for index in range(chunks):
                numbers = jnp.stack([jnp.int32(0), here[1], jnp.int32(0)])
                state = attend(
                    numbers, ranges_turned, block_position, q, [rows[index]],
                    [(index, (0,))], state, index == chunks - 1, group_size, 1, chunk,
                )
            outs.append(state[0])
            square = square + state[1]
        outs = [jnp.concatenate(outs, axis=1)]
    square = lax.psum(square, "head")
    return pl.pallas_call(
        functools.partial(finish_kernel, split),
        in_specs=[SMEM, SMEM] + [VMEM] * (2 + split),
        out_specs=VMEM,
        out_shape=jax.ShapeDtypeStruct(queries.shape, BF16),
    )(here, noise_ids, square, level_gain, *outs)


def solution(mesh):
    placed = (P("ctx", "head"), P("ctx", "head"), P("ctx", "head"), P(), P(), P(), P(None, "head"))
    return jax.shard_map(
        body, mesh=mesh, in_specs=placed, out_specs=P("ctx", "head"), check_vma=False
    )
```

```python
import functools

import jax
import jax.numpy as jnp
from jax import lax
from jax.experimental import pallas as pl
from jax.experimental.pallas import tpu as pltpu
from jax.sharding import PartitionSpec as P

D = 6144
HD = 128
BLK = 128
STRETCHES = 4
LOG2E = 1.4426950408889634
NEGATIVE = -1e30

F32 = jnp.float32
BF16 = jnp.bfloat16
VMEM = pl.BlockSpec(memory_space=pltpu.VMEM)
SMEM = pl.BlockSpec(memory_space=pltpu.SMEM)
ROOM = 52 * 1024 * 1024
ROOM_SMALL = 38 * 1024 * 1024


def attend_kernel(spec, *refs):
    sources, split, per_device, pieces, group_size, first, last, nr = spec
    where_ref, ranges_ref, position_ref = refs[:3]
    at = 3
    query_refs = refs[at : at + pieces]
    at += pieces
    row_refs = refs[at : at + len(sources)]
    at += len(sources)
    if not first:
        acc_in, stat_in = refs[at : at + 2]
        at += 2
    if last:
        out_refs, square_refs = refs[at : at + pieces], refs[at + pieces : at + 2 * pieces]
        at += 2 * pieces
    else:
        acc_out, stat_out = refs[at : at + 2]
        at += 2
    kept_k, kept_v, score_ref, acc_ref = refs[at : at + 4]
    at += 4
    if not first:
        acc_old, stat_old, semaphores = refs[at : at + 3]
        fetches = [
            pltpu.make_async_copy(acc_in, acc_old, semaphores.at[0]),
            pltpu.make_async_copy(stat_in, stat_old, semaphores.at[1]),
        ]
        for fetch in fetches:
            fetch.start()
    q_rows = query_refs[0].shape[0]
    width = pieces * q_rows * group_size
    to_log2 = LOG2E / HD**0.5

    place, stretch, group = where_ref[0], where_ref[1], where_ref[2]
    count = jnp.int32(0)
    for index, (bits, steps) in enumerate(sources):
        held = jnp.bitwise_xor(group, bits)
        for at_step, step in enumerate(steps):
            device = held * split + jnp.bitwise_xor(place, step)
            for block in range(per_device):
                logical = position_ref[device * per_device + block]
                live = jnp.bool_(False)
                for r in range(nr):
                    low, high = ranges_ref[r, 0, stretch], ranges_ref[r, 1, stretch]
                    live = live | ((logical >= low) & (logical < high))

                @pl.when(live)
                def _(count=count, index=index, slot=2 * at_step * per_device + block):
                    kept_k[count] = row_refs[index][slot]
                    kept_v[count] = row_refs[index][slot + per_device]

                count = count + live.astype(jnp.int32)
    kept_v[count] = jnp.zeros((BLK, HD), BF16)

    pairs = lax.div(count, 2)
    quads = lax.div(count, 4)
    q = jnp.concatenate(
        [ref[:, g * HD : (g + 1) * HD] for ref in query_refs for g in range(group_size)], axis=0
    )
    acc_ref[:, :HD] = jnp.full((width, HD), NEGATIVE, F32)

    def scores(start, blocks):
        keys = kept_k[pl.ds(start, blocks)].reshape(blocks * BLK, HD)
        score = lax.dot_general(q, keys, (((1,), (1,)), ((), ())), preferred_element_type=F32)
        top = score[:, :BLK]
        for b in range(1, blocks):
            top = jnp.maximum(top, score[:, b * BLK : (b + 1) * BLK])
        acc_ref[:, :HD] = jnp.maximum(acc_ref[:, :HD], top)
        return score

    def quad_scores(index, carry):
        score = scores(index * 4, 4)
        score_ref[index * 2] = score[:, : 2 * BLK]
        score_ref[index * 2 + 1] = score[:, 2 * BLK :]
        return carry

    def pair_scores(index, carry):
        score_ref[index] = scores(index * 2, 2)
        return carry

    lax.fori_loop(0, quads, quad_scores, 0)
    lax.fori_loop(quads * 2, pairs, pair_scores, 0)

    @pl.when(count > pairs * 2)
    def _():
        score_ref[pairs, :, :BLK] = scores(count - 1, 1)
        score_ref[pairs, :, BLK:] = jnp.full((width, BLK), NEGATIVE, F32)

    top = jnp.max(acc_ref[:, :HD], axis=1, keepdims=True) * to_log2
    if not first:
        for fetch in fetches:
            fetch.wait()
        old_top = stat_old[:, :1]
        top = jnp.maximum(top, old_top)
        correct = jnp.exp2(old_top - top)
        acc_ref[:, :HD] = acc_old[...] * correct
        acc_ref[:, HD:] = jnp.broadcast_to(stat_old[:, HD // 2 : HD // 2 + 1] * correct, (width, HD))
    else:
        acc_ref[...] = jnp.zeros((width, 2 * HD), F32)
    top_wide = jnp.broadcast_to(top, (width, 2 * BLK))

    def sums(start, number):
        weight = jnp.concatenate(
            [jnp.exp2(score_ref[start + i] * to_log2 - top_wide).astype(BF16) for i in range(number)], axis=1
        )
        values = kept_v[pl.ds(start * 2, number * 2)].reshape(number * 2 * BLK, HD)
        values = jnp.concatenate([values, jnp.ones((number * 2 * BLK, HD), BF16)], axis=1)
        acc_ref[...] += jnp.dot(weight, values, preferred_element_type=F32)

    def quad_sums(index, carry):
        sums(index * 2, 2)
        return carry

    def pair_sums(index, carry):
        sums(index, 1)
        return carry

    steps = lax.div(count + 1, 2)
    twice = lax.div(steps, 2)
    lax.fori_loop(0, twice, quad_sums, 0)
    lax.fori_loop(twice * 2, steps, pair_sums, 0)
    if last:
        heads = acc_ref[:, :HD] / acc_ref[:, HD:]
        for p in range(pieces):
            square = jnp.zeros((q_rows, HD), F32)
            for g in range(group_size):
                start = (p * group_size + g) * q_rows
                part = heads[start : start + q_rows]
                square = square + part * part
                out_refs[p][:, g * HD : (g + 1) * HD] = part.astype(BF16)
            square = jnp.sum(square, axis=1, keepdims=True)
            square_refs[p][...] = jnp.broadcast_to(square, (q_rows, q_rows)).T[:8]
    else:
        acc_out[...] = acc_ref[:, :HD]
        lane = lax.broadcasted_iota(jnp.int32, (width, HD), 1)
        stat_out[...] = jnp.where(lane < HD // 2, jnp.broadcast_to(top, (width, HD)), acc_ref[:, HD:])


def attend(where, ranges, position, q, row_list, sources, state, last, group_size, split, per_device):
    pieces = len(q)
    q_rows = q[0].shape[0]
    width = pieces * q_rows * group_size
    nr = ranges.shape[0]
    first = state is None
    most = sum(rows.shape[0] for rows in row_list) // 2
    spec = (tuple(sources), split, per_device, pieces, group_size, first, last, nr)
    if last:
        shapes = [jax.ShapeDtypeStruct(q[0].shape, BF16)] * pieces + [jax.ShapeDtypeStruct((8, q_rows), F32)] * pieces
    else:
        shapes = [jax.ShapeDtypeStruct((width, HD), F32)] * 2
    inputs = len(sources) + pieces
    held = [] if first else [pltpu.VMEM((width, HD), F32)] * 2 + [pltpu.SemaphoreType.DMA((2,))]
    return pl.pallas_call(
        functools.partial(attend_kernel, spec),
        in_specs=[SMEM] * 3 + [VMEM] * inputs + [pl.BlockSpec(memory_space=pl.ANY)] * (0 if first else 2),
        out_specs=[VMEM] * len(shapes),
        out_shape=shapes,
        scratch_shapes=[
            pltpu.VMEM((most + 2, BLK, HD), BF16),
            pltpu.VMEM((most + 2, BLK, HD), BF16),
            pltpu.VMEM((most // 2 + 1, width, 2 * BLK), F32),
            pltpu.VMEM((width, 2 * HD), F32),
            *held,
        ],
        compiler_params=pltpu.CompilerParams(vmem_limit_bytes=ROOM if most > 8 else ROOM_SMALL),
        cost_estimate=pl.CostEstimate(
            flops=12 * width * most * BLK * HD, bytes_accessed=4 * width * HD, transcendentals=width * most * BLK
        ),
    )(where, ranges, position, *q, *row_list, *(() if first else state))


def pieces_kernel(split, inputs, where_ref, *refs):
    for step in range(split):
        row = 0
        for source in refs[:inputs]:
            rows, width = source.shape[0], source.shape[1] // split
            start = pl.multiple_of(jnp.bitwise_xor(where_ref[0], step) * width, HD)
            refs[len(refs) - split + step][row : row + rows] = source[:, pl.ds(start, width)]
            row += rows


def pieces_of(where, split, arrays, *before):
    rows = sum(array.shape[0] for array in arrays)
    shapes = [jax.ShapeDtypeStruct((rows, arrays[0].shape[1] // split), arrays[0].dtype)] * split
    return pl.pallas_call(
        functools.partial(pieces_kernel, split, len(arrays)),
        in_specs=[SMEM] + [VMEM] * len(arrays) + [pl.BlockSpec(memory_space=pl.ANY)] * len(before),
        out_specs=[VMEM] * split,
        out_shape=shapes,
    )(where, *arrays, *before)


def copy_kernel(rows_ref, before_ref, out_ref):
    out_ref[...] = rows_ref[...]


def copy_after(rows, before):
    return pl.pallas_call(
        copy_kernel,
        in_specs=[VMEM, pl.BlockSpec(memory_space=pl.ANY)],
        out_specs=VMEM,
        out_shape=jax.ShapeDtypeStruct(rows.shape, rows.dtype),
    )(rows, before)


def finish_kernel(split, where_ref, noise_ref, square_ref, gain_ref, *refs):
    out_ref = refs[split]
    q_rows, width = refs[0].shape
    level = noise_ref[where_ref[1]]
    square = jnp.broadcast_to(square_ref[:1], (q_rows, q_rows)).T[:, :1]
    scale = 1.0 / jnp.sqrt(square / D + 1e-06)
    for step in range(split):
        start = pl.multiple_of(jnp.bitwise_xor(where_ref[0], step) * width, HD)
        gain = gain_ref[pl.ds(level, 1), pl.ds(start, width)]
        out_ref[:, pl.ds(start, width)] = (refs[step][...].astype(F32) * scale * gain).astype(BF16)


def body(queries, keys, values, ranges, noise_ids, block_position, level_gain):
    devices = lax.axis_size("ctx")
    q_rows = queries.shape[0]
    heads_here = keys.shape[1] // HD
    group_size = queries.shape[1] // keys.shape[1]
    per_device = keys.shape[0] // BLK
    stretch_devices = devices // STRETCHES
    shared = heads_here == stretch_devices and heads_here & (heads_here - 1) == 0 and STRETCHES & (STRETCHES - 1) == 0
    split = heads_here if shared else 1
    groups = devices // split
    me = lax.axis_index("ctx")
    here = jnp.stack([lax.rem(me, split), lax.div(me, stretch_devices), lax.div(me, split)]).astype(jnp.int32)
    ranges_turned = ranges.transpose(1, 2, 0)

    def permute(array, pairs):
        return lax.ppermute(array, "ctx", pairs)

    def within(step):
        return [(i, i ^ step) for i in range(devices)]

    def between(bits):
        return [(i, (i // split ^ bits) * split + i % split) for i in range(devices)]

    if shared:
        row_pieces = pieces_of(here, split, [keys, values])
        query_pieces = pieces_of(here, split, [queries])
        got = [row_pieces[0]] + [permute(row_pieces[step], within(step)) for step in range(1, split)]
        halves = [range(split // 2), range(split // 2, split)]
        have = [
            (0, steps, jnp.concatenate([got[step] for step in steps], axis=0).reshape(-1, BLK, HD)) for steps in halves
        ]
        q = [query_pieces[0]] + [permute(query_pieces[step], within(step)) for step in range(1, split)]
        reach = groups
        while reach > 1:
            arrived = []
            for bits, steps, rows in have:
                if reach == groups and arrived:
                    rows = copy_after(rows, arrived[-1][2])
                    turned = (bits, steps, rows)
                arrived.append((bits ^ (reach - 1), steps, permute(rows, between(reach - 1))))
            have += arrived
            reach //= 2
        have[1] = turned
        order = [0] + sorted({source[0] for source in have if source[0]}, key=lambda bits: (bits == have[-1][0], bits))
        phases = [[source for source in have if source[0] == bits] for bits in order]
        state = None
        for index, phase in enumerate(phases):
            state = attend(
                here, ranges_turned, block_position, q, [rows for _, _, rows in phase],
                [(bits, tuple(steps)) for bits, steps, _ in phase], state, index == len(phases) - 1,
                group_size, split, per_device,
            )
        outs, squares = state[:split], state[split:]
        square = squares[0]
        for step in range(1, split):
            square = square + permute(squares[step], within(step))
        outs = [outs[0]] + [permute(outs[step], within(step)) for step in range(1, split)]
    else:
        key_all = lax.all_gather(keys, "ctx", axis=0, tiled=True)
        value_all = lax.all_gather(values, "ctx", axis=0, tiled=True)
        chunk = min(32, key_all.shape[0] // BLK)
        outs, square = [], 0.0
        for head in range(heads_here):
            columns = slice(head * HD, (head + 1) * HD)
            q = [queries[:, head * group_size * HD : (head + 1) * group_size * HD]]
            rows = [array[:, columns].reshape(-1, chunk, BLK, HD) for array in (key_all, value_all)]
            rows = jnp.concatenate(rows, axis=1)
            state, chunks = None, rows.shape[0]
            for index in range(chunks):
                numbers = jnp.stack([jnp.int32(0), here[1], jnp.int32(0)])
                state = attend(
                    numbers, ranges_turned, block_position, q, [rows[index]],
                    [(index, (0,))], state, index == chunks - 1, group_size, 1, chunk,
                )
            outs.append(state[0])
            square = square + state[1]
        outs = [jnp.concatenate(outs, axis=1)]
    square = lax.psum(square, "head")
    return pl.pallas_call(
        functools.partial(finish_kernel, split),
        in_specs=[SMEM, SMEM] + [VMEM] * (2 + split),
        out_specs=VMEM,
        out_shape=jax.ShapeDtypeStruct(queries.shape, BF16),
    )(here, noise_ids, square, level_gain, *outs)


def solution(mesh):
    placed = (P("ctx", "head"), P("ctx", "head"), P("ctx", "head"), P(), P(), P(), P(None, "head"))
    return jax.shard_map(
        body, mesh=mesh, in_specs=placed, out_specs=P("ctx", "head"), check_vma=False
    )
```

```python
import functools

import jax
import jax.numpy as jnp
from jax import lax
from jax.experimental import pallas as pl
from jax.experimental.pallas import tpu as pltpu
from jax.sharding import PartitionSpec as P

D = 6144
HD = 128
BLK = 128
STRETCHES = 4
LOG2E = 1.4426950408889634
NEGATIVE = -1e30

F32 = jnp.float32
BF16 = jnp.bfloat16
VMEM = pl.BlockSpec(memory_space=pltpu.VMEM)
SMEM = pl.BlockSpec(memory_space=pltpu.SMEM)
ROOM = 52 * 1024 * 1024
ROOM_SMALL = 38 * 1024 * 1024


def attend_kernel(spec, *refs):
    sources, split, per_device, pieces, group_size, first, last, nr = spec
    where_ref, ranges_ref, position_ref = refs[:3]
    at = 3
    query_refs = refs[at : at + pieces]
    at += pieces
    row_refs = refs[at : at + len(sources)]
    at += len(sources)
    if not first:
        acc_in, stat_in = refs[at : at + 2]
        at += 2
    if last:
        out_refs, square_ref = refs[at : at + pieces], refs[at + pieces]
        at += pieces + 1
    else:
        acc_out, stat_out = refs[at : at + 2]
        at += 2
    kept_k, kept_v, score_ref, acc_ref = refs[at : at + 4]
    at += 4
    if not first:
        acc_old, stat_old, semaphores = refs[at : at + 3]
        fetches = [
            pltpu.make_async_copy(acc_in, acc_old, semaphores.at[0]),
            pltpu.make_async_copy(stat_in, stat_old, semaphores.at[1]),
        ]
        for fetch in fetches:
            fetch.start()
    q_rows = query_refs[0].shape[0]
    width = pieces * q_rows * group_size
    to_log2 = LOG2E / HD**0.5

    place, stretch, group = where_ref[0], where_ref[1], where_ref[2]
    count = jnp.int32(0)
    for index, (bits, steps) in enumerate(sources):
        held = jnp.bitwise_xor(group, bits)
        for at_step, step in enumerate(steps):
            device = held * split + jnp.bitwise_xor(place, step)
            for block in range(per_device):
                logical = position_ref[device * per_device + block]
                live = jnp.bool_(False)
                for r in range(nr):
                    low, high = ranges_ref[r, 0, stretch], ranges_ref[r, 1, stretch]
                    live = live | ((logical >= low) & (logical < high))

                @pl.when(live)
                def _(count=count, index=index, slot=2 * at_step * per_device + block):
                    kept_k[count] = row_refs[index][slot]
                    kept_v[count] = row_refs[index][slot + per_device]

                count = count + live.astype(jnp.int32)
    kept_v[count] = jnp.zeros((BLK, HD), BF16)

    pairs = lax.div(count, 2)
    quads = lax.div(count, 4)
    q = jnp.concatenate(
        [ref[:, g * HD : (g + 1) * HD] for ref in query_refs for g in range(group_size)], axis=0
    )
    acc_ref[:, :HD] = jnp.full((width, HD), NEGATIVE, F32)

    def scores(start, blocks):
        keys = kept_k[pl.ds(start, blocks)].reshape(blocks * BLK, HD)
        score = lax.dot_general(q, keys, (((1,), (1,)), ((), ())), preferred_element_type=F32)
        top = score[:, :BLK]
        for b in range(1, blocks):
            top = jnp.maximum(top, score[:, b * BLK : (b + 1) * BLK])
        acc_ref[:, :HD] = jnp.maximum(acc_ref[:, :HD], top)
        return score

    def quad_scores(index, carry):
        score = scores(index * 4, 4)
        score_ref[index * 2] = score[:, : 2 * BLK]
        score_ref[index * 2 + 1] = score[:, 2 * BLK :]
        return carry

    def pair_scores(index, carry):
        score_ref[index] = scores(index * 2, 2)
        return carry

    lax.fori_loop(0, quads, quad_scores, 0)
    lax.fori_loop(quads * 2, pairs, pair_scores, 0)

    @pl.when(count > pairs * 2)
    def _():
        score_ref[pairs, :, :BLK] = scores(count - 1, 1)
        score_ref[pairs, :, BLK:] = jnp.full((width, BLK), NEGATIVE, F32)

    top = jnp.max(acc_ref[:, :HD], axis=1, keepdims=True) * to_log2
    if not first:
        for fetch in fetches:
            fetch.wait()
        old_top = stat_old[:, :1]
        top = jnp.maximum(top, old_top)
        correct = jnp.exp2(old_top - top)
        acc_ref[:, :HD] = acc_old[...] * correct
        acc_ref[:, HD:] = jnp.broadcast_to(stat_old[:, HD // 2 : HD // 2 + 1] * correct, (width, HD))
    else:
        acc_ref[...] = jnp.zeros((width, 2 * HD), F32)
    top_wide = jnp.broadcast_to(top, (width, 2 * BLK))

    def sums(start, number):
        weight = jnp.concatenate(
            [jnp.exp2(score_ref[start + i] * to_log2 - top_wide).astype(BF16) for i in range(number)], axis=1
        )
        values = kept_v[pl.ds(start * 2, number * 2)].reshape(number * 2 * BLK, HD)
        values = jnp.concatenate([values, jnp.ones((number * 2 * BLK, HD), BF16)], axis=1)
        acc_ref[...] += jnp.dot(weight, values, preferred_element_type=F32)

    def quad_sums(index, carry):
        sums(index * 2, 2)
        return carry

    def pair_sums(index, carry):
        sums(index, 1)
        return carry

    steps = lax.div(count + 1, 2)
    twice = lax.div(steps, 2)
    lax.fori_loop(0, twice, quad_sums, 0)
    lax.fori_loop(twice * 2, steps, pair_sums, 0)
    if last:
        heads = acc_ref[:, :HD] / acc_ref[:, HD:]
        for p in range(pieces):
            square = jnp.zeros((q_rows, HD), F32)
            for g in range(group_size):
                start = (p * group_size + g) * q_rows
                part = heads[start : start + q_rows]
                square = square + part * part
                out_refs[p][:, g * HD : (g + 1) * HD] = part.astype(BF16)
            square = jnp.sum(square, axis=1, keepdims=True)
            square_ref[p * 8 : (p + 1) * 8] = jnp.broadcast_to(square, (q_rows, q_rows)).T[:8]
    else:
        acc_out[...] = acc_ref[:, :HD]
        lane = lax.broadcasted_iota(jnp.int32, (width, HD), 1)
        stat_out[...] = jnp.where(lane < HD // 2, jnp.broadcast_to(top, (width, HD)), acc_ref[:, HD:])


def attend(where, ranges, position, q, row_list, sources, state, last, group_size, split, per_device):
    pieces = len(q)
    q_rows = q[0].shape[0]
    width = pieces * q_rows * group_size
    nr = ranges.shape[0]
    first = state is None
    most = sum(rows.shape[0] for rows in row_list) // 2
    spec = (tuple(sources), split, per_device, pieces, group_size, first, last, nr)
    if last:
        shapes = [jax.ShapeDtypeStruct(q[0].shape, BF16)] * pieces + [jax.ShapeDtypeStruct((8 * pieces, q_rows), F32)]
    else:
        shapes = [jax.ShapeDtypeStruct((width, HD), F32)] * 2
    inputs = len(sources) + pieces
    held = [] if first else [pltpu.VMEM((width, HD), F32)] * 2 + [pltpu.SemaphoreType.DMA((2,))]
    return pl.pallas_call(
        functools.partial(attend_kernel, spec),
        in_specs=[SMEM] * 3 + [VMEM] * inputs + [pl.BlockSpec(memory_space=pl.ANY)] * (0 if first else 2),
        out_specs=[VMEM] * len(shapes),
        out_shape=shapes,
        scratch_shapes=[
            pltpu.VMEM((most + 2, BLK, HD), BF16),
            pltpu.VMEM((most + 2, BLK, HD), BF16),
            pltpu.VMEM((most // 2 + 1, width, 2 * BLK), F32),
            pltpu.VMEM((width, 2 * HD), F32),
            *held,
        ],
        compiler_params=pltpu.CompilerParams(vmem_limit_bytes=ROOM if most > 8 else ROOM_SMALL),
        cost_estimate=pl.CostEstimate(
            flops=12 * width * most * BLK * HD, bytes_accessed=4 * width * HD, transcendentals=width * most * BLK
        ),
    )(where, ranges, position, *q, *row_list, *(() if first else state))


def pieces_kernel(split, inputs, where_ref, *refs):
    for step in range(split):
        row = 0
        for source in refs[:inputs]:
            rows, width = source.shape[0], source.shape[1] // split
            start = pl.multiple_of(jnp.bitwise_xor(where_ref[0], step) * width, HD)
            refs[len(refs) - split + step][row : row + rows] = source[:, pl.ds(start, width)]
            row += rows


def pieces_of(where, split, arrays, *before):
    rows = sum(array.shape[0] for array in arrays)
    shapes = [jax.ShapeDtypeStruct((rows, arrays[0].shape[1] // split), arrays[0].dtype)] * split
    return pl.pallas_call(
        functools.partial(pieces_kernel, split, len(arrays)),
        in_specs=[SMEM] + [VMEM] * len(arrays) + [pl.BlockSpec(memory_space=pl.ANY)] * len(before),
        out_specs=[VMEM] * split,
        out_shape=shapes,
    )(where, *arrays, *before)


def copy_kernel(rows_ref, before_ref, out_ref):
    out_ref[...] = rows_ref[...]


def copy_after(rows, before):
    return pl.pallas_call(
        copy_kernel,
        in_specs=[VMEM, pl.BlockSpec(memory_space=pl.ANY)],
        out_specs=VMEM,
        out_shape=jax.ShapeDtypeStruct(rows.shape, rows.dtype),
    )(rows, before)


def finish_kernel(split, where_ref, noise_ref, gain_ref, *refs):
    square_refs, out_ref = refs[split:-1], refs[-1]
    q_rows, width = refs[0].shape
    level = noise_ref[where_ref[1]]
    square = sum(ref[:1] for ref in square_refs)
    square = jnp.broadcast_to(square, (q_rows, q_rows)).T[:, :1]
    scale = 1.0 / jnp.sqrt(square / D + 1e-06)
    for step in range(split):
        start = pl.multiple_of(jnp.bitwise_xor(where_ref[0], step) * width, HD)
        gain = gain_ref[pl.ds(level, 1), pl.ds(start, width)]
        out_ref[:, pl.ds(start, width)] = (refs[step][...].astype(F32) * scale * gain).astype(BF16)


def body(queries, keys, values, ranges, noise_ids, block_position, level_gain):
    devices = lax.axis_size("ctx")
    columns = lax.axis_size("head")
    q_rows = queries.shape[0]
    heads_here = keys.shape[1] // HD
    group_size = queries.shape[1] // keys.shape[1]
    per_device = keys.shape[0] // BLK
    stretch_devices = devices // STRETCHES
    shared = heads_here == stretch_devices and heads_here & (heads_here - 1) == 0 and STRETCHES & (STRETCHES - 1) == 0
    split = heads_here if shared else 1
    groups = devices // split
    me = lax.axis_index("ctx")
    here = jnp.stack([lax.rem(me, split), lax.div(me, stretch_devices), lax.div(me, split)]).astype(jnp.int32)
    ranges_turned = ranges.transpose(1, 2, 0)

    def permute(array, pairs):
        return lax.ppermute(array, "ctx", pairs)

    def within(step):
        return [(i, i ^ step) for i in range(devices)]

    def between(bits):
        return [(i, (i // split ^ bits) * split + i % split) for i in range(devices)]

    if shared:
        row_pieces = pieces_of(here, split, [keys, values])
        query_pieces = pieces_of(here, split, [queries])
        got = [row_pieces[0]] + [permute(row_pieces[step], within(step)) for step in range(1, split)]
        halves = [range(split // 2), range(split // 2, split)]
        have = [
            (0, steps, jnp.concatenate([got[step] for step in steps], axis=0).reshape(-1, BLK, HD)) for steps in halves
        ]
        q = [query_pieces[0]] + [permute(query_pieces[step], within(step)) for step in range(1, split)]
        reach = groups
        while reach > 1:
            arrived = []
            for bits, steps, rows in have:
                if reach == groups and arrived:
                    rows = copy_after(rows, arrived[-1][2])
                    turned = (bits, steps, rows)
                arrived.append((bits ^ (reach - 1), steps, permute(rows, between(reach - 1))))
            have += arrived
            reach //= 2
        have[1] = turned
        order = [0] + sorted({source[0] for source in have if source[0]}, key=lambda bits: (bits == have[-1][0], bits))
        phases = [[source for source in have if source[0] == bits] for bits in order]
        state = None
        for index, phase in enumerate(phases):
            state = attend(
                here, ranges_turned, block_position, q, [rows for _, _, rows in phase],
                [(bits, tuple(steps)) for bits, steps, _ in phase], state, index == len(phases) - 1,
                group_size, split, per_device,
            )
        outs, squares = state[:split], [state[split][8 * step : 8 * step + 8] for step in range(split)]
        square = squares[0]
        for step in range(1, split):
            square = square + permute(squares[step], within(step))
        outs = [outs[0]] + [permute(outs[step], within(step)) for step in range(1, split)]
    else:
        key_all = lax.all_gather(keys, "ctx", axis=0, tiled=True)
        value_all = lax.all_gather(values, "ctx", axis=0, tiled=True)
        chunk = min(32, key_all.shape[0] // BLK)
        outs, square = [], 0.0
        for head in range(heads_here):
            own = slice(head * HD, (head + 1) * HD)
            q = [queries[:, head * group_size * HD : (head + 1) * group_size * HD]]
            rows = [array[:, own].reshape(-1, chunk, BLK, HD) for array in (key_all, value_all)]
            rows = jnp.concatenate(rows, axis=1)
            state, chunks = None, rows.shape[0]
            for index in range(chunks):
                numbers = jnp.stack([jnp.int32(0), here[1], jnp.int32(0)])
                state = attend(
                    numbers, ranges_turned, block_position, q, [rows[index]],
                    [(index, (0,))], state, index == chunks - 1, group_size, 1, chunk,
                )
            outs.append(state[0])
            square = square + state[1]
        outs = [jnp.concatenate(outs, axis=1)]
    if columns == 2:
        squares = [square, lax.ppermute(square, "head", [(0, 1), (1, 0)])]
    else:
        squares = [lax.psum(square, "head")]
    return pl.pallas_call(
        functools.partial(finish_kernel, split),
        in_specs=[SMEM, SMEM] + [VMEM] * (1 + split + len(squares)),
        out_specs=VMEM,
        out_shape=jax.ShapeDtypeStruct(queries.shape, BF16),
    )(here, noise_ids, level_gain, *outs, *squares)


def solution(mesh):
    placed = (P("ctx", "head"), P("ctx", "head"), P("ctx", "head"), P(), P(), P(), P(None, "head"))
    return jax.shard_map(
        body, mesh=mesh, in_specs=placed, out_specs=P("ctx", "head"), check_vma=False
    )
```
